32 devices in a mesh: section: 2 (over y), scene: 4 (over z), mp: 4 (over x, core).
Axes of the slice: x: 2, y: 2, z: 4, core: 2. Of those that a mesh axis runs over, the one named last changes fastest.
Arguments:
- dec_grad: bfloat16 [4, 8, 256, 4096], P('scene', ('section', 'mp')), may hold values from -2.109375 to 2.109375
- agent_queries: bfloat16 [4, 256, 4096], P('scene', None, ('section', 'mp')), as said below
- map_keys: bfloat16 [4, 1024, 4096], P('scene', None, ('section', 'mp')), as said below
- map_values: bfloat16 [4, 1024, 4096], P('scene', None, ('section', 'mp')), may hold values from -6 to 6
- w_out: bfloat16 [4096, 4096], P(('section', 'mp'), 'scene'), may hold values from -0.09375 to 0.09375
- block_mask: int32 [4, 2, 8], P('scene'), may hold values from 0 to 1, as said below
- agent_count: int32 [4], P('scene'), may hold values from 64 to 256
Outputs:
- d_queries: bfloat16 [4, 256, 4096], P('scene', None, ('section', 'mp'))
- d_keys: bfloat16 [4, 1024, 4096], P('scene', None, ('section', 'mp'))
- d_values: bfloat16 [4, 1024, 4096], P('scene', None, ('section', 'mp'))
- d_wout: float32 [4096, 4096], P(('section', 'mp'), 'scene')
The draws below stay inside these ranges and needn't reach their ends.
Inputs may be any that keep to these rules, and one draw needn't show every extreme that they name: `block_mask`: every agent block of a scene sees map block 0. In each scene at most 4 map blocks are seen by some agent block, and some scene reaches 4. `agent_queries`: entries are finite and of moderate size. `map_keys`: entries are finite and of moderate size.
All inputs are finite; a program needn't handle non-finite values.
Results may differ from the reference program's by a relative error of at most 0.04.
Values may be sent and summed in bfloat16 or wider, within the bound.
A program may use at most 64 MiB of HBM per device.

```python
import math
import jax
import jax.numpy as jnp
from jax import lax

D = 4096
HEAD_DIM = 128
HEADS = 32
BLOCK = 128
AGENT_TOK = 256
MAP_TOK = 1024
SAMP_DEV = 1
SAMPLES = 8
SCENES = 4
QBLOCKS = 2
MBLOCKS = 8
MAXLIVE = 4
N_SECTION = 2
N_MP = 4


def draw_agent_queries(key, part):
    base = jax.random.truncated_normal(jax.random.fold_in(key, 1), -6.0, 6.0, (SCENES, AGENT_TOK, D), jnp.float32)
    return base.astype(jnp.bfloat16)


def draw_map_keys(key, part):
    base = jax.random.truncated_normal(jax.random.fold_in(key, 2), -6.0, 6.0, (SCENES, MAP_TOK, D), jnp.float32)
    return base.astype(jnp.bfloat16)


def draw_block_mask(key, part):
    live_count = jax.random.randint(jax.random.fold_in(key, 11), (SCENES,), max(MAXLIVE // 2, 1), MAXLIVE + 1)
    fullest = jax.random.randint(jax.random.fold_in(key, 12), (), 0, SCENES)
    live_count = jnp.where(jnp.arange(SCENES) == fullest, MAXLIVE, live_count)
    scene_keys = jax.random.split(jax.random.fold_in(key, 13), SCENES)
    shuffled = jax.vmap(lambda one_key: jax.random.permutation(one_key, MBLOCKS - 1))(scene_keys)
    ranking = jnp.argsort(shuffled, axis=1)
    chosen = ranking < live_count[:, None] - 1
    union = jnp.concatenate([jnp.ones((SCENES, 1), dtype=bool), chosen], axis=1)
    coins = jax.random.randint(jax.random.fold_in(key, 14), (SCENES, QBLOCKS, MBLOCKS), 0, 2) == 1
    block_ids = jnp.arange(MBLOCKS)
    owner = block_ids[None, :] % QBLOCKS == jnp.arange(QBLOCKS)[:, None]
    forced = owner | (block_ids == 0)[None, :]
    visible = union[:, None, :] & (coins | forced[None])
    return visible.astype(jnp.int32)


def place_ends(drawn, key, low, top_value):
    extent = drawn.shape
    spot = [jax.random.randint(jax.random.fold_in(key, axis), (), 0, extent[axis]) for axis in range(len(extent))]
    drawn = drawn.at[tuple(spot)].set(low)
    longest = extent.index(max(extent))
    spot[longest] = (spot[longest] + 1) % extent[longest]
    return drawn.at[tuple(spot)].set(top_value)


def level_of(stream_key, dims, cuts, smallest, high):
    level = 1.0
    for position, blocks in cuts:
        draws = jax.random.uniform(jax.random.fold_in(jax.random.fold_in(stream_key, 6), position), (blocks,), jnp.float32, smallest / len(cuts), high / len(cuts))
        level = level * jnp.repeat(jnp.exp(draws), dims[position] // blocks).reshape((-1,) + (1,) * (len(dims) - 1 - position))
    return level


def scatter_about(own_key, dims, scale, reach, pieces=(), kind=jnp.bfloat16):
    drawn = scale * jax.random.normal(own_key, dims, jnp.float32)
    if pieces:
        drawn = drawn * level_of(own_key, dims, pieces, -0.22, 0.18)
    return jnp.clip(drawn, -reach, reach).astype(kind)


def setup_inputs(seed: int = 0) -> dict:
    keys = jax.random.split(jax.random.key(seed), 8)
    return {
        "dec_grad": scatter_about(keys[0], (SCENES, SAMPLES, AGENT_TOK, D), (SAMPLES ** -0.5), 2.109375, ((0, 4), (1, 8))),
        "agent_queries": draw_agent_queries(jax.random.fold_in(keys[7], 71), 0),
        "map_keys": draw_map_keys(jax.random.fold_in(keys[7], 71), 0),
        "map_values": scatter_about(keys[3], (SCENES, MAP_TOK, D), 1.0, 6.0, ((0, 4), (2, 8))),
        "w_out": scatter_about(keys[4], (D, D), D ** -0.5, 0.09375, ((0, 8), (1, 4))),
        "block_mask": draw_block_mask(jax.random.fold_in(keys[7], 71), 0),
        "agent_count": place_ends(jax.random.randint(keys[6], (SCENES,), AGENT_TOK // 4, AGENT_TOK + 1), jax.random.fold_in(keys[6], 1), AGENT_TOK // 4, AGENT_TOK).astype(jnp.int32),
    }


def reference(dec_grad, agent_queries, map_keys, map_values, w_out, block_mask, agent_count):
    device_groups = N_SECTION * N_MP
    scaling = 1.0 / math.sqrt(HEAD_DIM)

    def one_scene(weight_grad, inputs):
        sample_grads, queries, key_rows, value_rows, mask_rows, agent_total = inputs
        grouped = sample_grads.reshape(device_groups, SAMP_DEV, AGENT_TOK, D).astype(jnp.float32)
        partial_value = lax.optimization_barrier(jnp.sum(grouped, axis=1)).astype(jnp.bfloat16)
        summed = lax.optimization_barrier(jnp.sum(partial_value.astype(jnp.float32), axis=0))
        row_keep = jnp.arange(AGENT_TOK) < agent_total
        upstream = jnp.where(row_keep[:, None], summed, 0.0).astype(jnp.bfloat16)
        d_attn = jnp.dot(upstream, w_out.T, preferred_element_type=jnp.float32).astype(jnp.bfloat16)
        visible = jnp.repeat(jnp.repeat(mask_rows == 1, BLOCK, axis=0), BLOCK, axis=1)
        query_heads = queries.reshape(AGENT_TOK, HEADS, HEAD_DIM).astype(jnp.float32)
        key_heads = key_rows.reshape(MAP_TOK, HEADS, HEAD_DIM).astype(jnp.float32)
        value_heads = value_rows.reshape(MAP_TOK, HEADS, HEAD_DIM).astype(jnp.float32)
        grad_heads = d_attn.reshape(AGENT_TOK, HEADS, HEAD_DIM).astype(jnp.float32)
        scores = jnp.einsum('qhd,khd->hqk', query_heads, key_heads) * scaling
        scores = jnp.where(visible[None], scores, -1e+30)
        largest = lax.optimization_barrier(jnp.max(scores, axis=-1, keepdims=True))
        exponent = jnp.exp(scores - largest)
        probs = exponent / lax.optimization_barrier(jnp.sum(exponent, axis=-1, keepdims=True))
        weights = lax.optimization_barrier(probs.astype(jnp.bfloat16)).astype(jnp.float32)
        attended = jnp.einsum('hqk,khd->qhd', weights, value_heads)
        attended_rounded = attended.astype(jnp.bfloat16)
        weight_grad = weight_grad + jnp.dot(attended_rounded.reshape(AGENT_TOK, D).T, upstream, preferred_element_type=jnp.float32)
        delta = lax.optimization_barrier(jnp.sum(grad_heads * attended, axis=-1))
        d_values = jnp.einsum('hqk,qhd->khd', weights, grad_heads).astype(jnp.bfloat16)
        d_probs = jnp.einsum('qhd,khd->hqk', grad_heads, value_heads)
        d_scores = probs * (d_probs - delta.T[:, :, None])
        score_grads = lax.optimization_barrier(d_scores.astype(jnp.bfloat16)).astype(jnp.float32)
        d_queries = (scaling * jnp.einsum('hqk,khd->qhd', score_grads, key_heads)).astype(jnp.bfloat16)
        d_keys = (scaling * jnp.einsum('hqk,qhd->khd', score_grads, query_heads)).astype(jnp.bfloat16)
        return (weight_grad, (d_queries.reshape(AGENT_TOK, D), d_keys.reshape(MAP_TOK, D), d_values.reshape(MAP_TOK, D)))
    initial = jnp.zeros((D, D), jnp.float32)
    d_wout, outputs = lax.scan(one_scene, initial, (dec_grad, agent_queries, map_keys, map_values, block_mask, agent_count))
    d_queries, d_keys, d_values = outputs
    return (d_queries, d_keys, d_values, d_wout)
```

```python
import functools
import math

import jax
import jax.numpy as jnp
from jax import lax
from jax.experimental import pallas as pl
from jax.experimental.pallas import tpu as pltpu
from jax.sharding import PartitionSpec as P

HEAD_DIM = 128


def attend_forward(query_heads, key_heads, value_heads, visible, scaling):
    scores = (
        jnp.einsum("qhd,khd->hqk", query_heads, key_heads, preferred_element_type=jnp.float32)
        * scaling
    )
    scores = jnp.where(visible[None], scores, -1e30)
    largest = jnp.max(scores, axis=-1, keepdims=True)
    exponent = jnp.exp(scores - largest)
    probs = exponent / jnp.sum(exponent, axis=-1, keepdims=True)
    weights = probs.astype(jnp.bfloat16)
    attended = jnp.einsum("hqk,khd->qhd", weights, value_heads, preferred_element_type=jnp.float32)
    return (probs, weights, attended)


def attend_backward(
    query_heads, key_heads, value_heads, grad_heads, probs, weights, attended, scaling
):
    delta = jnp.sum(grad_heads.astype(jnp.float32) * attended, axis=-1)
    d_values = jnp.einsum(
        "hqk,qhd->khd", weights, grad_heads, preferred_element_type=jnp.float32
    ).astype(jnp.bfloat16)
    d_probs = jnp.einsum(
        "qhd,khd->hqk", grad_heads, value_heads, preferred_element_type=jnp.float32
    )
    score_grads = (probs * (d_probs - delta.T[:, :, None])).astype(jnp.bfloat16)
    d_queries = (
        scaling
        * jnp.einsum("hqk,khd->qhd", score_grads, key_heads, preferred_element_type=jnp.float32)
    ).astype(jnp.bfloat16)
    d_keys = (
        scaling
        * jnp.einsum("hqk,qhd->khd", score_grads, query_heads, preferred_element_type=jnp.float32)
    ).astype(jnp.bfloat16)
    return (d_queries, d_keys, d_values)


def reduce_weights(attended_rounded, upstream):
    term = jnp.einsum("qh,qd->hd", attended_rounded, upstream, preferred_element_type=jnp.float32)
    return lax.psum_scatter(term, "scene", scatter_dimension=1, tiled=True)


def shards(dec_grad, agent_queries, map_keys, map_values, w_out, block_mask, agent_count):
    scaling = 1.0 / math.sqrt(HEAD_DIM)
    partial_sum = jnp.sum(dec_grad[0].astype(jnp.float32), axis=0).astype(jnp.bfloat16)
    agent_total = agent_count[0]
    token_rows = partial_sum.shape[0]
    summed = lax.psum(partial_sum, ("section", "mp")).astype(jnp.float32)
    row_keep = jnp.arange(token_rows) < agent_total
    upstream = jnp.where(row_keep[:, None], summed, 0.0).astype(jnp.bfloat16)
    proj_width = w_out.shape[0]
    d_attn = jnp.einsum(
        "td,hd->th",
        upstream,
        lax.all_gather(w_out, "scene", axis=1, tiled=True),
        preferred_element_type=jnp.float32,
    ).astype(jnp.bfloat16)
    head_count = proj_width // HEAD_DIM
    query_heads = agent_queries[0].reshape(token_rows, head_count, HEAD_DIM)
    grad_heads = d_attn.reshape(token_rows, head_count, HEAD_DIM)
    key_rows = map_keys[0]
    value_rows = map_values[0]
    mask_rows = block_mask[0]
    map_blocks = mask_rows.shape[1]
    block_size = key_rows.shape[0] // map_blocks
    visible = jnp.repeat(jnp.repeat(mask_rows == 1, block_size, axis=0), block_size, axis=1)
    key_heads = key_rows.reshape(-1, head_count, HEAD_DIM)
    value_heads = value_rows.reshape(-1, head_count, HEAD_DIM)
    probs, weights, attended = attend_forward(query_heads, key_heads, value_heads, visible, scaling)
    attended_rounded = attended.astype(jnp.bfloat16).reshape(token_rows, proj_width)
    d_queries, d_keys, d_values = attend_backward(
        query_heads, key_heads, value_heads, grad_heads, probs, weights, attended, scaling
    )
    d_wout = reduce_weights(attended_rounded, upstream)
    d_keys_out = d_keys.reshape(-1, proj_width)
    d_values_out = d_values.reshape(-1, proj_width)
    return (
        d_queries.reshape(token_rows, proj_width)[None],
        d_keys_out[None],
        d_values_out[None],
        d_wout,
    )


def attention_kernel(
    scenes, dec_ref, q_ref, k_ref, v_ref, w_ref, mask_ref, count_ref,
    dq_ref, dk_ref, dv_ref, dw_ref,
    core_in, acc, half_in, acc_half, quarter_in, piece, up, att_all, attended, probs,
    part_out, part_in, part_own, grads,
    core_sem, half_sem, quarter_sem, swap_send, swap_recv, g1_send, g1_recv, g2_send, g2_recv,
    g3_send, g3_recv, att_send, att_recv, part_send, part_recv,
):
    z, y, m = lax.axis_index("scene"), lax.axis_index("section"), lax.axis_index("mp")
    x, c = lax.div(m, 2), lax.rem(m, 2)
    core_peer, x_peer, y_peer = {"mp": m + 1 - 2 * c}, {"mp": m + 2 - 4 * x}, {"section": 1 - y}
    rows, width = q_ref.shape[1], q_ref.shape[2]
    half, quarter, eighth = rows // 2, rows // 4, rows // 8
    cols = w_ref.shape[1]
    lane = cols // 2
    heads = width // HEAD_DIM
    scaling = 1.0 / math.sqrt(HEAD_DIM)
    map_blocks, q_blocks = mask_ref.shape[2], mask_ref.shape[1]
    map_block, q_block = k_ref.shape[1] // map_blocks, rows // q_blocks

    def remote(src, dst, send, recv, peer):
        return pltpu.make_async_remote_copy(
            src_ref=src, dst_ref=dst, send_sem=send, recv_sem=recv, device_id=peer,
            device_id_type=pl.DeviceIdType.MESH,
        )

    def span(start, size):
        return pl.ds(pl.multiple_of(start, size), size)

    def scene_at(step):
        return lax.rem(z + step, scenes)

    barrier = pltpu.get_barrier_semaphore()
    peers = [core_peer, x_peer, y_peer] + [{"scene": scene_at(d)} for d in range(1, scenes)]
    for peer in peers:
        pl.semaphore_signal(barrier, inc=1, device_id=peer, device_id_type=pl.DeviceIdType.MESH)
    pl.semaphore_wait(barrier, len(peers))

    def forward(h, carry):
        head = span(h * HEAD_DIM, HEAD_DIM)
        for qb in range(q_blocks):
            block = pl.ds(qb * q_block, q_block)
            scores = lax.dot_general(
                q_ref[0, block, head], k_ref[0, :, head], (((1,), (1,)), ((), ())),
                preferred_element_type=jnp.float32,
            ) * scaling
            hidden = jnp.concatenate(
                [
                    jnp.full((1, map_block), jnp.where(mask_ref[0, qb, mb] == 1, 0.0, -1e30), jnp.float32)
                    for mb in range(map_blocks)
                ],
                axis=1,
            )
            scores = scores + hidden
            exponent = jnp.exp(scores - jnp.max(scores, axis=-1, keepdims=True))
            prob = exponent / jnp.sum(exponent, axis=-1, keepdims=True)
            probs[h, block, :] = prob
            value = jnp.dot(
                prob.astype(jnp.bfloat16), v_ref[0, :, head], preferred_element_type=jnp.float32
            )
            attended[block, head] = value
            att_all[z, block, head] = value.astype(jnp.bfloat16)
        return carry

    def add(a, b):
        return (a.astype(jnp.float32) + b.astype(jnp.float32)).astype(jnp.bfloat16)

    first = remote(
        dec_ref.at[0, 0, span((1 - c) * half, half), :], core_in, core_sem.at[0], core_sem.at[1],
        core_peer,
    )
    first.start()
    lax.fori_loop(0, 1, forward, 0)
    first.wait()
    for s in range(scenes):
        for l in range(2):
            at = pl.ds(s * cols + l * lane, lane)
            acc[l, :, pl.ds(s * lane, lane)] = add(
                dec_ref[0, 0, span(c * half, half), at], core_in[:, at]
            )
    bits = ((x, y), (y, x))
    order = ((x_peer, y_peer), (y_peer, x_peer))
    copies = [
        remote(
            acc.at[l, span((1 - bits[l][0]) * quarter, quarter), :], half_in.at[l],
            half_sem.at[0, l], half_sem.at[1, l], order[l][0],
        )
        for l in range(2)
    ]
    for copy in copies:
        copy.start()
    lax.fori_loop(1, heads, forward, 0)

    def move_attended(step, wait_only):
        for way, sign in ((0, 1), (1, -1)):
            slot = z - sign * step
            there = (slot >= 0) if sign == 1 else (slot < scenes)
            onward = (z < scenes - 1) if sign == 1 else (z > 0)

            @pl.when(jnp.logical_and(there, onward) if step == 0 or wait_only else there)
            def _():
                copy = remote(
                    att_all.at[slot], att_all.at[slot], att_send.at[way, step], att_recv.at[slot],
                    {"scene": z + sign},
                )
                if wait_only:
                    copy.wait_send()
                elif step == 0:
                    copy.start()
                else:
                    copy.wait_recv()
                    pl.when(onward)(lambda: copy.start())

    move_attended(0, False)
    for copy in copies:
        copy.wait()
    copies = []
    for l in range(2):
        acc_half[l] = add(acc[l, span(bits[l][0] * quarter, quarter), :], half_in[l])
        copies.append(
            remote(
                acc_half.at[l, span((1 - bits[l][1]) * eighth, eighth), :], quarter_in.at[l],
                quarter_sem.at[0, l], quarter_sem.at[1, l], order[l][1],
            )
        )
        copies[l].start()
    starts = [c * half + bits[l][0] * quarter + bits[l][1] * eighth for l in range(2)]
    places = [span(starts[l], eighth) for l in range(2)]
    for l in range(2):
        copies[l].wait()
        total = add(acc_half[l, span(bits[l][1] * eighth, eighth), :], quarter_in[l])
        row = starts[l] + lax.broadcasted_iota(jnp.int32, total.shape, 0)
        total = jnp.where(row < count_ref[0], total.astype(jnp.float32), 0.0).astype(jnp.bfloat16)
        for s in range(scenes):
            piece[s, l] = total[:, s * lane : (s + 1) * lane]
        up[z, l, places[l], :] = piece[z, l]

    def swap(d, l):
        to = scene_at(d)
        return remote(
            piece.at[to, l], up.at[z, l, places[l], :], swap_send.at[d, l], swap_recv.at[d, l],
            {"scene": to},
        )

    for d in range(1, scenes):
        for l in range(2):
            swap(d, l).start()

    def block_of(d, l, size, lead):
        return up.at[scene_at(scenes - d), l, span(lead, size), :]

    def gather_one(d, l, sides=(g1_send, g1_recv)):
        ref = block_of(d, l, eighth, starts[l])
        return remote(ref, ref, sides[0].at[d, l], sides[1].at[d, l], order[l][1])

    def gather_two(d, l):
        ref = block_of(d, l, quarter, c * half + bits[l][0] * quarter)
        return remote(ref, ref, g2_send.at[d, l], g2_recv.at[d, l], order[l][0])

    def gather_three(d):
        ref = up.at[scene_at(scenes - d), :, span(c * half, half), :]
        return remote(ref, ref, g3_send.at[d], g3_recv.at[d], core_peer)

    def landed_one(d, l):
        other = c * half + bits[l][0] * quarter + (1 - bits[l][1]) * eighth
        ref = block_of(d, l, eighth, other)
        return remote(ref, ref, g1_send.at[d, l], g1_recv.at[d, l], order[l][1])

    def landed_two(d, l):
        ref = block_of(d, l, quarter, c * half + (1 - bits[l][0]) * quarter)
        return remote(ref, ref, g2_send.at[d, l], g2_recv.at[d, l], order[l][0])

    def landed_three(d):
        ref = up.at[scene_at(scenes - d), :, span((1 - c) * half, half), :]
        return remote(ref, ref, g3_send.at[d], g3_recv.at[d], core_peer)

    def send_part(d):
        return remote(
            part_out.at[d], part_in.at[d], part_send.at[d], part_recv.at[d],
            {"scene": scene_at(scenes - d)},
        )

    for t in range(scenes + 3):
        if t < scenes:
            for l in range(2):
                if t > 0:
                    remote(
                        piece.at[0, l], up.at[scene_at(scenes - t), l, places[l], :],
                        swap_send.at[t, l], swap_recv.at[t, l], {"scene": scene_at(t)},
                    ).wait_recv()
                gather_one(t, l).start()
        if t == 1:
            for step in range(1, scenes - 1):
                move_attended(step, False)
        if 0 <= t - 1 < scenes:
            for l in range(2):
                landed_one(t - 1, l).wait_recv()
                gather_two(t - 1, l).start()
        if 0 <= t - 2 < scenes:
            for l in range(2):
                landed_two(t - 2, l).wait_recv()
            gather_three(t - 2).start()
        if t >= 3:
            d = t - 3
            landed_three(d).wait_recv()
            slot = scene_at(scenes - d)
            part = sum(
                lax.dot_general(
                    up[slot, l], w_ref[:, l * lane : (l + 1) * lane], (((1,), (1,)), ((), ())),
                    preferred_element_type=jnp.float32,
                )
                for l in range(2)
            )
            if d == 0:
                part_own[...] = part
            else:
                part_out[d] = part.astype(jnp.bfloat16)
                send_part(d).start()

    move_attended(scenes - 1, False)

    def weight_columns(tile, carry):
        for l in range(2):
            size = lane // 2
            at = span(tile * size, size)
            dw_ref[:, span(l * lane + tile * size, size)] = sum(
                lax.dot_general(
                    att_all[s], up[s, l, :, at], (((0,), (0,)), ((), ())),
                    preferred_element_type=jnp.float32,
                )
                for s in range(scenes)
            )
        return carry

    lax.fori_loop(0, 2, weight_columns, 0)

    total = part_own[...]
    for d in range(1, scenes):
        send_part(d).wait_recv()
        total = total + part_in[d].astype(jnp.float32)
    grads[...] = total.astype(jnp.bfloat16)

    def backward(h, carry):
        head = span(h * HEAD_DIM, HEAD_DIM)
        grad = grads[:, head]
        prob = probs[h]
        delta = jnp.sum(grad.astype(jnp.float32) * attended[:, head], axis=-1, keepdims=True)
        dv_ref[0, :, head] = lax.dot_general(
            prob.astype(jnp.bfloat16), grad, (((0,), (0,)), ((), ())),
            preferred_element_type=jnp.float32,
        ).astype(jnp.bfloat16)
        d_probs = lax.dot_general(
            grad, v_ref[0, :, head], (((1,), (1,)), ((), ())), preferred_element_type=jnp.float32
        )
        score_grads = (prob * (d_probs - delta)).astype(jnp.bfloat16)
        dq_ref[0, :, head] = (
            scaling
            * jnp.dot(score_grads, k_ref[0, :, head], preferred_element_type=jnp.float32)
        ).astype(jnp.bfloat16)
        dk_ref[0, :, head] = (
            scaling
            * lax.dot_general(
                score_grads, q_ref[0, :, head], (((0,), (0,)), ((), ())),
                preferred_element_type=jnp.float32,
            )
        ).astype(jnp.bfloat16)
        return carry

    lax.fori_loop(0, heads, backward, 0)

    for step in range(scenes - 1):
        move_attended(step, True)
    for d in range(scenes):
        for l in range(2):
            if d > 0:
                swap(d, l).wait_send()
            gather_one(d, l).wait_send()
            gather_two(d, l).wait_send()
        gather_three(d).wait_send()
        if d > 0:
            send_part(d).wait_send()


def fused_shards(scenes, dec_grad, agent_queries, map_keys, map_values, w_out, block_mask, agent_count):
    rows, width = agent_queries.shape[1:]
    map_rows = map_keys.shape[1]
    model = dec_grad.shape[3]
    cols = w_out.shape[1]
    lane, packed = cols // 2, model // 2
    heads = width // HEAD_DIM
    bf16, f32 = jnp.bfloat16, jnp.float32
    vmem, smem = pl.BlockSpec(memory_space=pltpu.VMEM), pl.BlockSpec(memory_space=pltpu.SMEM)
    dma = pltpu.SemaphoreType.DMA
    return pl.pallas_call(
        functools.partial(attention_kernel, scenes),
        out_shape=(
            jax.ShapeDtypeStruct((1, rows, width), bf16),
            jax.ShapeDtypeStruct((1, map_rows, width), bf16),
            jax.ShapeDtypeStruct((1, map_rows, width), bf16),
            jax.ShapeDtypeStruct((width, cols), f32),
        ),
        in_specs=[vmem] * 5 + [smem] * 2,
        out_specs=(vmem,) * 4,
        scratch_shapes=[
            pltpu.VMEM((rows // 2, model), bf16),
            pltpu.VMEM((2, rows // 2, packed), bf16),
            pltpu.VMEM((2, rows // 4, packed), bf16),
            pltpu.VMEM((2, rows // 4, packed), bf16),
            pltpu.VMEM((2, rows // 8, packed), bf16),
            pltpu.VMEM((scenes, 2, rows // 8, lane), bf16),
            pltpu.VMEM((scenes, 2, rows, lane), bf16),
            pltpu.VMEM((scenes, rows, width), bf16),
            pltpu.VMEM((rows, width), f32),
            pltpu.VMEM((heads, rows, map_rows), f32),
            pltpu.VMEM((scenes, rows, width), bf16),
            pltpu.VMEM((scenes, rows, width), bf16),
            pltpu.VMEM((rows, width), f32),
            pltpu.VMEM((rows, width), bf16),
            dma((2,)),
            dma((2, 2)),
            dma((2, 2)),
            dma((scenes, 2)),
            dma((scenes, 2)),
            dma((scenes, 2)),
            dma((scenes, 2)),
            dma((scenes, 2)),
            dma((scenes, 2)),
            dma((scenes,)),
            dma((scenes,)),
            dma((2, scenes)),
            dma((scenes,)),
            dma((scenes,)),
            dma((scenes,)),
        ],
        compiler_params=pltpu.CompilerParams(
            collective_id=0, has_side_effects=True, vmem_limit_bytes=50 * 1024 * 1024
        ),
    )(dec_grad, agent_queries, map_keys, map_values, w_out, block_mask, agent_count)


def solution(mesh):
    scenes = mesh.shape["scene"]

    def body(dec_grad, agent_queries, map_keys, map_values, w_out, block_mask, agent_count):
        args = (dec_grad, agent_queries, map_keys, map_values, w_out, block_mask, agent_count)
        fits = (
            (mesh.shape["section"], mesh.shape["mp"], dec_grad.shape[1]) == (2, 4, 1)
            and scenes >= 2
            and dec_grad.shape[2] % 128 == 0
            and w_out.shape[1] % 512 == 0
        )
        return functools.partial(fused_shards, scenes)(*args) if fits else shards(*args)

    return jax.shard_map(
        body,
        mesh=mesh,
        in_specs=(
            P("scene", ("section", "mp"), None, None),
            P("scene", None, ("section", "mp")),
            P("scene", None, ("section", "mp")),
            P("scene", None, ("section", "mp")),
            P(("section", "mp"), "scene"),
            P("scene", None, None),
            P("scene"),
        ),
        out_specs=(
            P("scene", None, ("section", "mp")),
            P("scene", None, ("section", "mp")),
            P("scene", None, ("section", "mp")),
            P(("section", "mp"), "scene"),
        ),
        check_vma=False,
    )
```

```python
import functools
import math

import jax
import jax.numpy as jnp
from jax import lax
from jax.experimental import pallas as pl
from jax.experimental.pallas import tpu as pltpu
from jax.sharding import PartitionSpec as P

HEAD_DIM = 128


def attend_forward(query_heads, key_heads, value_heads, visible, scaling):
    scores = (
        jnp.einsum("qhd,khd->hqk", query_heads, key_heads, preferred_element_type=jnp.float32)
        * scaling
    )
    scores = jnp.where(visible[None], scores, -1e30)
    largest = jnp.max(scores, axis=-1, keepdims=True)
    exponent = jnp.exp(scores - largest)
    probs = exponent / jnp.sum(exponent, axis=-1, keepdims=True)
    weights = probs.astype(jnp.bfloat16)
    attended = jnp.einsum("hqk,khd->qhd", weights, value_heads, preferred_element_type=jnp.float32)
    return (probs, weights, attended)


def attend_backward(
    query_heads, key_heads, value_heads, grad_heads, probs, weights, attended, scaling
):
    delta = jnp.sum(grad_heads.astype(jnp.float32) * attended, axis=-1)
    d_values = jnp.einsum(
        "hqk,qhd->khd", weights, grad_heads, preferred_element_type=jnp.float32
    ).astype(jnp.bfloat16)
    d_probs = jnp.einsum(
        "qhd,khd->hqk", grad_heads, value_heads, preferred_element_type=jnp.float32
    )
    score_grads = (probs * (d_probs - delta.T[:, :, None])).astype(jnp.bfloat16)
    d_queries = (
        scaling
        * jnp.einsum("hqk,khd->qhd", score_grads, key_heads, preferred_element_type=jnp.float32)
    ).astype(jnp.bfloat16)
    d_keys = (
        scaling
        * jnp.einsum("hqk,qhd->khd", score_grads, query_heads, preferred_element_type=jnp.float32)
    ).astype(jnp.bfloat16)
    return (d_queries, d_keys, d_values)


def reduce_weights(attended_rounded, upstream):
    term = jnp.einsum("qh,qd->hd", attended_rounded, upstream, preferred_element_type=jnp.float32)
    return lax.psum_scatter(term, "scene", scatter_dimension=1, tiled=True)


def shards(dec_grad, agent_queries, map_keys, map_values, w_out, block_mask, agent_count):
    scaling = 1.0 / math.sqrt(HEAD_DIM)
    partial_sum = jnp.sum(dec_grad[0].astype(jnp.float32), axis=0).astype(jnp.bfloat16)
    agent_total = agent_count[0]
    token_rows = partial_sum.shape[0]
    summed = lax.psum(partial_sum, ("section", "mp")).astype(jnp.float32)
    row_keep = jnp.arange(token_rows) < agent_total
    upstream = jnp.where(row_keep[:, None], summed, 0.0).astype(jnp.bfloat16)
    proj_width = w_out.shape[0]
    d_attn = jnp.einsum(
        "td,hd->th",
        upstream,
        lax.all_gather(w_out, "scene", axis=1, tiled=True),
        preferred_element_type=jnp.float32,
    ).astype(jnp.bfloat16)
    head_count = proj_width // HEAD_DIM
    query_heads = agent_queries[0].reshape(token_rows, head_count, HEAD_DIM)
    grad_heads = d_attn.reshape(token_rows, head_count, HEAD_DIM)
    key_rows = map_keys[0]
    value_rows = map_values[0]
    mask_rows = block_mask[0]
    map_blocks = mask_rows.shape[1]
    block_size = key_rows.shape[0] // map_blocks
    visible = jnp.repeat(jnp.repeat(mask_rows == 1, block_size, axis=0), block_size, axis=1)
    key_heads = key_rows.reshape(-1, head_count, HEAD_DIM)
    value_heads = value_rows.reshape(-1, head_count, HEAD_DIM)
    probs, weights, attended = attend_forward(query_heads, key_heads, value_heads, visible, scaling)
    attended_rounded = attended.astype(jnp.bfloat16).reshape(token_rows, proj_width)
    d_queries, d_keys, d_values = attend_backward(
        query_heads, key_heads, value_heads, grad_heads, probs, weights, attended, scaling
    )
    d_wout = reduce_weights(attended_rounded, upstream)
    d_keys_out = d_keys.reshape(-1, proj_width)
    d_values_out = d_values.reshape(-1, proj_width)
    return (
        d_queries.reshape(token_rows, proj_width)[None],
        d_keys_out[None],
        d_values_out[None],
        d_wout,
    )


def attention_kernel(
    scenes, dec_hbm, q_hbm, k_hbm, v_hbm, w_hbm, mask_ref, count_ref,
    dq_hbm, dk_hbm, dv_hbm, dw_hbm,
    dec_ref, q_ref, k_ref, v_ref, w_ref, dq_ref, dk_ref, dv_ref, dw_ref,
    core_in, acc, half_in, acc_half, quarter_in, piece, up, att_all, attended, probs,
    parts, part_out, part_in, part_own, grads,
    load_sem, store_sem, core_send, core_recv, half_send, half_recv, quarter_send, quarter_recv,
    swap_send, swap_recv, g1_send, g1_recv, g2_send, g2_recv,
    g3_send, g3_recv, att_send, att_recv, part_send, part_recv,
):
    z, y, m = lax.axis_index("scene"), lax.axis_index("section"), lax.axis_index("mp")
    x, c = lax.div(m, 2), lax.rem(m, 2)
    core_peer, x_peer, y_peer = {"mp": m + 1 - 2 * c}, {"mp": m + 2 - 4 * x}, {"section": 1 - y}
    rows, width = q_ref.shape[1], q_ref.shape[2]
    half, quarter, eighth = rows // 2, rows // 4, rows // 8
    cols = w_ref.shape[1]
    lane = cols // 2
    heads = width // HEAD_DIM
    scaling = 1.0 / math.sqrt(HEAD_DIM)
    map_blocks, q_blocks = mask_ref.shape[2], mask_ref.shape[1]
    map_block, q_block = k_ref.shape[1] // map_blocks, rows // q_blocks

    def remote(src, dst, send, recv, peer):
        return pltpu.make_async_remote_copy(
            src_ref=src, dst_ref=dst, send_sem=send, recv_sem=recv, device_id=peer,
            device_id_type=pl.DeviceIdType.MESH,
        )

    def span(start, size):
        return pl.ds(pl.multiple_of(start, size), size)

    def partner(r):
        high, low = lax.div(z, 2), lax.rem(z, 2)
        return 2 * (1 - high if r & 2 else high) + (1 - low if r & 1 else low)

    rounds = [r for r in range(scenes - 1, -1, -1)]
    targets = [partner(r) for r in rounds]

    loads = [
        pltpu.make_async_copy(src, dst, load_sem.at[i])
        for i, (src, dst) in enumerate(
            (
                (q_hbm, q_ref), (k_hbm, k_ref), (v_hbm, v_ref), (w_hbm, w_ref),
                (dec_hbm.at[0, 0, span(c * half, half), :], dec_ref),
            )
        )
    ]
    for load in loads:
        load.start()

    barrier = pltpu.get_barrier_semaphore()
    peers = [core_peer, x_peer, y_peer] + [{"scene": targets[j]} for j in range(scenes - 1)]
    for peer in peers:
        pl.semaphore_signal(barrier, inc=1, device_id=peer, device_id_type=pl.DeviceIdType.MESH)
    pl.semaphore_wait(barrier, len(peers))

    def core_copy(j):
        return remote(
            dec_hbm.at[0, 0, span((1 - c) * half, half), span(targets[j] * cols, cols)],
            core_in.at[j], core_send.at[j], core_recv.at[j], core_peer,
        )

    for j in range(scenes):
        core_copy(j).start()

    def forward(h, carry):
        head = span(h * HEAD_DIM, HEAD_DIM)
        for qb in range(q_blocks):
            block = pl.ds(qb * q_block, q_block)
            scores = lax.dot_general(
                q_ref[0, block, head], k_ref[0, :, head], (((1,), (1,)), ((), ())),
                preferred_element_type=jnp.float32,
            ) * scaling
            hidden = jnp.concatenate(
                [
                    jnp.full((1, map_block), jnp.where(mask_ref[0, qb, mb] == 1, 0.0, -1e30), jnp.float32)
                    for mb in range(map_blocks)
                ],
                axis=1,
            )
            scores = scores + hidden
            exponent = jnp.exp(scores - jnp.max(scores, axis=-1, keepdims=True))
            prob = exponent / jnp.sum(exponent, axis=-1, keepdims=True)
            probs[h, block, :] = prob
            value = jnp.dot(
                prob.astype(jnp.bfloat16), v_ref[0, :, head], preferred_element_type=jnp.float32
            )
            attended[block, head] = value
            att_all[z, block, head] = value.astype(jnp.bfloat16)
        return carry

    def add(a, b):
        return (a.astype(jnp.float32) + b.astype(jnp.float32)).astype(jnp.bfloat16)

    def move_attended(step, wait_only):
        for way, sign in ((0, 1), (1, -1)):
            slot = z - sign * step
            there = (slot >= 0) if sign == 1 else (slot < scenes)
            onward = (z < scenes - 1) if sign == 1 else (z > 0)

            @pl.when(jnp.logical_and(there, onward) if step == 0 or wait_only else there)
            def _():
                copy = remote(
                    att_all.at[slot], att_all.at[slot], att_send.at[way, step], att_recv.at[slot],
                    {"scene": z + sign},
                )
                if wait_only:
                    copy.wait_send()
                elif step == 0:
                    copy.start()
                else:
                    copy.wait_recv()
                    pl.when(onward)(lambda: copy.start())

    bits = ((x, y), (y, x))
    order = ((x_peer, y_peer), (y_peer, x_peer))
    starts = [c * half + bits[l][0] * quarter + bits[l][1] * eighth for l in range(2)]
    places = [span(starts[l], eighth) for l in range(2)]

    def half_copy(j, l):
        return remote(
            acc.at[j, l, span((1 - bits[l][0]) * quarter, quarter), :], half_in.at[j, l],
            half_send.at[j, l], half_recv.at[j, l], order[l][0],
        )

    def quarter_copy(j, l):
        return remote(
            acc_half.at[j, l, span((1 - bits[l][1]) * eighth, eighth), :], quarter_in.at[j, l],
            quarter_send.at[j, l], quarter_recv.at[j, l], order[l][1],
        )

    def swap(j, l, slot):
        return remote(
            piece.at[j, l], up.at[slot, l, places[l], :], swap_send.at[j, l], swap_recv.at[j, l],
            {"scene": targets[j]},
        )

    def sum_core(j):
        core_copy(j).wait_recv()
        for l in range(2):
            mine = dec_ref[:, span(targets[j] * cols + l * lane, lane)]
            acc[j, l] = add(mine, core_in[j, :, l * lane : (l + 1) * lane])
            half_copy(j, l).start()

    def sum_half(j):
        for l in range(2):
            half_copy(j, l).wait_recv()
            acc_half[j, l] = add(acc[j, l, span(bits[l][0] * quarter, quarter), :], half_in[j, l])
            quarter_copy(j, l).start()

    def sum_quarter(j):
        for l in range(2):
            quarter_copy(j, l).wait_recv()
            total = add(acc_half[j, l, span(bits[l][1] * eighth, eighth), :], quarter_in[j, l])
            row = starts[l] + lax.broadcasted_iota(jnp.int32, total.shape, 0)
            total = jnp.where(row < count_ref[0], total.astype(jnp.float32), 0.0)
            if j < scenes - 1:
                piece[j, l] = total.astype(jnp.bfloat16)
                swap(j, l, z).start()
            else:
                up[z, l, places[l], :] = total.astype(jnp.bfloat16)

    def gathered(j, l, size, lead, sems, peer):
        ref = up.at[targets[j], l, span(lead, size), :]
        return remote(ref, ref, sems[0].at[j, l], sems[1].at[j, l], peer)

    def gather_one(j, l, away=0):
        bit = 1 - bits[l][1] if away else bits[l][1]
        lead = c * half + bits[l][0] * quarter + bit * eighth
        return gathered(j, l, eighth, lead, (g1_send, g1_recv), order[l][1])

    def gather_two(j, l, away=0):
        bit = 1 - bits[l][0] if away else bits[l][0]
        return gathered(j, l, quarter, c * half + bit * quarter, (g2_send, g2_recv), order[l][0])

    def gather_three(j, away=0):
        core = 1 - c if away else c
        ref = up.at[targets[j], :, span(core * half, half), :]
        return remote(ref, ref, g3_send.at[j], g3_recv.at[j], core_peer)

    def spread_one(j):
        for l in range(2):
            if j < scenes - 1:
                swap(j, l, targets[j]).wait_recv()
            gather_one(j, l).start()

    def spread_two(j):
        for l in range(2):
            gather_one(j, l, 1).wait_recv()
            gather_two(j, l).start()

    def spread_three(j):
        for l in range(2):
            gather_two(j, l, 1).wait_recv()
        gather_three(j).start()

    def part_copy(j):
        t = targets[j]
        to = z + jnp.where(t > z, 1, -1)
        slot = jnp.where(jnp.logical_and(to == t, t < z), scenes, t)
        return remote(
            part_out.at[j], part_in.at[slot], part_send.at[j], part_recv.at[slot], {"scene": to}
        )

    def landed_part(slot):
        return remote(
            part_out.at[0], part_in.at[slot], part_send.at[0], part_recv.at[slot], core_peer
        )

    inner = jnp.logical_and(z > 0, z < scenes - 1)
    has_prev = [jnp.where(targets[j] > z, z, scenes - 1 - z) > 0 for j in range(scenes)]

    def multiply(j):
        gather_three(j, 1).wait_recv()
        t = targets[j]
        part = sum(
            lax.dot_general(
                up[t, l], w_ref[:, l * lane : (l + 1) * lane], (((1,), (1,)), ((), ())),
                preferred_element_type=jnp.float32,
            )
            for l in range(2)
        )
        if j == scenes - 1:
            part_own[...] = part
            return
        parts[j] = part

        @pl.when(jnp.logical_not(has_prev[j]))
        def _():
            part_out[j] = parts[j].astype(jnp.bfloat16)
            part_copy(j).start()

    def merge(j):
        @pl.when(has_prev[j])
        def _():
            landed_part(targets[j]).wait_recv()
            part_out[j] = (parts[j] + part_in[targets[j]].astype(jnp.float32)).astype(jnp.bfloat16)
            part_copy(j).start()

    stages = (
        sum_core, sum_half, sum_quarter, spread_one, spread_two, spread_three, multiply
    )
    loads[0].wait()
    loads[1].wait()
    loads[2].wait()
    forward(0, 0)
    loads[4].wait()
    for tick in range(scenes + len(stages) - 1):
        for lag, stage in enumerate(stages):
            if stage is multiply and tick == lag:
                loads[3].wait()
            if 0 <= tick - lag < scenes:
                stage(tick - lag)
        if tick + 1 < heads:
            forward(tick + 1, 0)
        if tick == heads - 2:
            move_attended(0, False)
        if tick == 5:
            move_attended(1, False)
        if tick == 7:
            move_attended(2, False)
        if tick == 8:
            merge(1)
        if tick == 9:
            merge(0)
    move_attended(scenes - 1, False)

    def weight_columns(tile, carry):
        for l in range(2):
            size = lane // 2
            at = span(tile * size, size)
            dw_ref[:, span(l * lane + tile * size, size)] = sum(
                lax.dot_general(
                    att_all[s], up[s, l, :, at], (((0,), (0,)), ((), ())),
                    preferred_element_type=jnp.float32,
                )
                for s in range(scenes)
            )
        return carry

    lax.fori_loop(0, 2, weight_columns, 0)

    store_dw = pltpu.make_async_copy(dw_ref, dw_hbm, store_sem.at[0])
    store_dw.start()
    merge(2)

    @pl.when(z > 0)
    def _():
        landed_part(z).wait_recv()
        part_own[...] = part_own[...] + part_in[z].astype(jnp.float32)

    @pl.when(z < scenes - 1)
    def _():
        landed_part(scenes).wait_recv()
        part_own[...] = part_own[...] + part_in[scenes].astype(jnp.float32)

    grads[...] = part_own[...].astype(jnp.bfloat16)

    def stores(h):
        head = span(h * HEAD_DIM, HEAD_DIM)
        return [
            pltpu.make_async_copy(src.at[0, :, head], dst.at[0, :, head], store_sem.at[1 + 3 * h + i])
            for i, (src, dst) in enumerate(((dq_ref, dq_hbm), (dk_ref, dk_hbm), (dv_ref, dv_hbm)))
        ]

    def backward(h, carry):
        head = span(h * HEAD_DIM, HEAD_DIM)
        grad = grads[:, head]
        prob = probs[h]
        delta = jnp.sum(grad.astype(jnp.float32) * attended[:, head], axis=-1, keepdims=True)
        dv_ref[0, :, head] = lax.dot_general(
            prob.astype(jnp.bfloat16), grad, (((0,), (0,)), ((), ())),
            preferred_element_type=jnp.float32,
        ).astype(jnp.bfloat16)
        d_probs = lax.dot_general(
            grad, v_ref[0, :, head], (((1,), (1,)), ((), ())), preferred_element_type=jnp.float32
        )
        score_grads = (prob * (d_probs - delta)).astype(jnp.bfloat16)
        dq_ref[0, :, head] = (
            scaling
            * jnp.dot(score_grads, k_ref[0, :, head], preferred_element_type=jnp.float32)
        ).astype(jnp.bfloat16)
        dk_ref[0, :, head] = (
            scaling
            * lax.dot_general(
                score_grads, q_ref[0, :, head], (((0,), (0,)), ((), ())),
                preferred_element_type=jnp.float32,
            )
        ).astype(jnp.bfloat16)
        return carry

    for h in range(heads):
        backward(h, 0)
        for store in stores(h):
            store.start()

    for step in range(scenes - 1):
        move_attended(step, True)
    for j in range(scenes):
        core_copy(j).wait_send()
        for l in range(2):
            half_copy(j, l).wait_send()
            quarter_copy(j, l).wait_send()
            gather_one(j, l).wait_send()
            gather_two(j, l).wait_send()
            if j < scenes - 1:
                swap(j, l, z).wait_send()
        gather_three(j).wait_send()
        if j < scenes - 1:
            part_copy(j).wait_send()
    store_dw.wait()
    for h in range(heads):
        for store in stores(h):
            store.wait()


def fused_shards(scenes, dec_grad, agent_queries, map_keys, map_values, w_out, block_mask, agent_count):
    rows, width = agent_queries.shape[1:]
    map_rows = map_keys.shape[1]
    model = dec_grad.shape[3]
    cols = w_out.shape[1]
    lane = cols // 2
    heads = width // HEAD_DIM
    bf16, f32 = jnp.bfloat16, jnp.float32
    anywhere, smem = pl.BlockSpec(memory_space=pl.ANY), pl.BlockSpec(memory_space=pltpu.SMEM)
    dma, vmem = pltpu.SemaphoreType.DMA, pltpu.VMEM
    return pl.pallas_call(
        functools.partial(attention_kernel, scenes),
        out_shape=(
            jax.ShapeDtypeStruct((1, rows, width), bf16),
            jax.ShapeDtypeStruct((1, map_rows, width), bf16),
            jax.ShapeDtypeStruct((1, map_rows, width), bf16),
            jax.ShapeDtypeStruct((width, cols), f32),
        ),
        in_specs=[anywhere] * 5 + [smem] * 2,
        out_specs=(anywhere,) * 4,
        scratch_shapes=[
            vmem((rows // 2, model), bf16),
            vmem((1, rows, width), bf16),
            vmem((1, map_rows, width), bf16),
            vmem((1, map_rows, width), bf16),
            vmem((width, cols), bf16),
            vmem((1, rows, width), bf16),
            vmem((1, map_rows, width), bf16),
            vmem((1, map_rows, width), bf16),
            vmem((width, cols), f32),
            vmem((scenes, rows // 2, cols), bf16),
            vmem((scenes, 2, rows // 2, lane), bf16),
            vmem((scenes, 2, rows // 4, lane), bf16),
            vmem((scenes, 2, rows // 4, lane), bf16),
            vmem((scenes, 2, rows // 8, lane), bf16),
            vmem((scenes, 2, rows // 8, lane), bf16),
            vmem((scenes, 2, rows, lane), bf16),
            vmem((scenes, rows, width), bf16),
            vmem((rows, width), f32),
            vmem((heads, rows, map_rows), f32),
            vmem((scenes, rows, width), f32),
            vmem((scenes, rows, width), bf16),
            vmem((scenes + 1, rows, width), bf16),
            vmem((rows, width), f32),
            vmem((rows, width), bf16),
            dma((5,)),
            dma((1 + 3 * heads,)),
            dma((scenes,)),
            dma((scenes,)),
            *[dma((scenes, 2))] * 10,
            dma((scenes,)),
            dma((scenes,)),
            dma((2, scenes)),
            dma((scenes,)),
            dma((scenes,)),
            dma((scenes + 1,)),
        ],
        compiler_params=pltpu.CompilerParams(
            collective_id=0, has_side_effects=True, vmem_limit_bytes=52 * 1024 * 1024
        ),
    )(dec_grad, agent_queries, map_keys, map_values, w_out, block_mask, agent_count)


def solution(mesh):
    scenes = mesh.shape["scene"]

    def body(dec_grad, agent_queries, map_keys, map_values, w_out, block_mask, agent_count):
        args = (dec_grad, agent_queries, map_keys, map_values, w_out, block_mask, agent_count)
        fits = (
            (mesh.shape["section"], mesh.shape["mp"], dec_grad.shape[1]) == (2, 4, 1)
            and scenes == 4
            and dec_grad.shape[2] % 128 == 0
            and w_out.shape[1] % 512 == 0
        )
        return functools.partial(fused_shards, scenes)(*args) if fits else shards(*args)

    return jax.shard_map(
        body,
        mesh=mesh,
        in_specs=(
            P("scene", ("section", "mp"), None, None),
            P("scene", None, ("section", "mp")),
            P("scene", None, ("section", "mp")),
            P("scene", None, ("section", "mp")),
            P(("section", "mp"), "scene"),
            P("scene", None, None),
            P("scene"),
        ),
        out_specs=(
            P("scene", None, ("section", "mp")),
            P("scene", None, ("section", "mp")),
            P("scene", None, ("section", "mp")),
            P(("section", "mp"), "scene"),
        ),
        check_vma=False,
    )
```

```python
import functools
import math

import jax
import jax.numpy as jnp
from jax import lax
from jax.experimental import pallas as pl
from jax.experimental.pallas import tpu as pltpu
from jax.sharding import PartitionSpec as P

HEAD_DIM = 128


def attend_forward(query_heads, key_heads, value_heads, visible, scaling):
    scores = (
        jnp.einsum("qhd,khd->hqk", query_heads, key_heads, preferred_element_type=jnp.float32)
        * scaling
    )
    scores = jnp.where(visible[None], scores, -1e30)
    largest = jnp.max(scores, axis=-1, keepdims=True)
    exponent = jnp.exp(scores - largest)
    probs = exponent / jnp.sum(exponent, axis=-1, keepdims=True)
    weights = probs.astype(jnp.bfloat16)
    attended = jnp.einsum("hqk,khd->qhd", weights, value_heads, preferred_element_type=jnp.float32)
    return (probs, weights, attended)


def attend_backward(
    query_heads, key_heads, value_heads, grad_heads, probs, weights, attended, scaling
):
    delta = jnp.sum(grad_heads.astype(jnp.float32) * attended, axis=-1)
    d_values = jnp.einsum(
        "hqk,qhd->khd", weights, grad_heads, preferred_element_type=jnp.float32
    ).astype(jnp.bfloat16)
    d_probs = jnp.einsum(
        "qhd,khd->hqk", grad_heads, value_heads, preferred_element_type=jnp.float32
    )
    score_grads = (probs * (d_probs - delta.T[:, :, None])).astype(jnp.bfloat16)
    d_queries = (
        scaling
        * jnp.einsum("hqk,khd->qhd", score_grads, key_heads, preferred_element_type=jnp.float32)
    ).astype(jnp.bfloat16)
    d_keys = (
        scaling
        * jnp.einsum("hqk,qhd->khd", score_grads, query_heads, preferred_element_type=jnp.float32)
    ).astype(jnp.bfloat16)
    return (d_queries, d_keys, d_values)


def reduce_weights(attended_rounded, upstream):
    term = jnp.einsum("qh,qd->hd", attended_rounded, upstream, preferred_element_type=jnp.float32)
    return lax.psum_scatter(term, "scene", scatter_dimension=1, tiled=True)


def shards(dec_grad, agent_queries, map_keys, map_values, w_out, block_mask, agent_count):
    scaling = 1.0 / math.sqrt(HEAD_DIM)
    partial_sum = jnp.sum(dec_grad[0].astype(jnp.float32), axis=0).astype(jnp.bfloat16)
    agent_total = agent_count[0]
    token_rows = partial_sum.shape[0]
    summed = lax.psum(partial_sum, ("section", "mp")).astype(jnp.float32)
    row_keep = jnp.arange(token_rows) < agent_total
    upstream = jnp.where(row_keep[:, None], summed, 0.0).astype(jnp.bfloat16)
    proj_width = w_out.shape[0]
    d_attn = jnp.einsum(
        "td,hd->th",
        upstream,
        lax.all_gather(w_out, "scene", axis=1, tiled=True),
        preferred_element_type=jnp.float32,
    ).astype(jnp.bfloat16)
    head_count = proj_width // HEAD_DIM
    query_heads = agent_queries[0].reshape(token_rows, head_count, HEAD_DIM)
    grad_heads = d_attn.reshape(token_rows, head_count, HEAD_DIM)
    key_rows = map_keys[0]
    value_rows = map_values[0]
    mask_rows = block_mask[0]
    map_blocks = mask_rows.shape[1]
    block_size = key_rows.shape[0] // map_blocks
    visible = jnp.repeat(jnp.repeat(mask_rows == 1, block_size, axis=0), block_size, axis=1)
    key_heads = key_rows.reshape(-1, head_count, HEAD_DIM)
    value_heads = value_rows.reshape(-1, head_count, HEAD_DIM)
    probs, weights, attended = attend_forward(query_heads, key_heads, value_heads, visible, scaling)
    attended_rounded = attended.astype(jnp.bfloat16).reshape(token_rows, proj_width)
    d_queries, d_keys, d_values = attend_backward(
        query_heads, key_heads, value_heads, grad_heads, probs, weights, attended, scaling
    )
    d_wout = reduce_weights(attended_rounded, upstream)
    d_keys_out = d_keys.reshape(-1, proj_width)
    d_values_out = d_values.reshape(-1, proj_width)
    return (
        d_queries.reshape(token_rows, proj_width)[None],
        d_keys_out[None],
        d_values_out[None],
        d_wout,
    )


def attention_kernel(
    scenes, dec_hbm, q_hbm, k_hbm, v_hbm, w_hbm, mask_ref, count_ref,
    dq_hbm, dk_hbm, dv_hbm, dw_hbm,
    dec_ref, q_ref, k_ref, v_ref, w_ref, dq_ref, dk_ref, dv_ref, dw_ref,
    core_in, acc, half_in, acc_half, quarter_in, piece, up, att_all, keys_t, probs,
    parts, part_out, part_in,
    load_sem, store_sem, core_send, core_recv, half_send, half_recv, quarter_send, quarter_recv,
    swap_send, swap_recv, g1_send, g1_recv, g2_send, g2_recv,
    g3_send, g3_recv, att_send, att_recv, part_send, part_recv,
):
    z, y, m = lax.axis_index("scene"), lax.axis_index("section"), lax.axis_index("mp")
    x, c = lax.div(m, 2), lax.rem(m, 2)
    core_peer, x_peer, y_peer = {"mp": m + 1 - 2 * c}, {"mp": m + 2 - 4 * x}, {"section": 1 - y}
    rows, width = q_ref.shape[1], q_ref.shape[2]
    half, quarter, eighth = rows // 2, rows // 4, rows // 8
    cols = w_ref.shape[1]
    lane = cols // 2
    heads = width // HEAD_DIM
    scaling = 1.0 / math.sqrt(HEAD_DIM)
    map_blocks, q_blocks = mask_ref.shape[2], mask_ref.shape[1]
    map_block, q_block = k_ref.shape[1] // map_blocks, rows // q_blocks

    def remote(src, dst, send, recv, peer):
        return pltpu.make_async_remote_copy(
            src_ref=src, dst_ref=dst, send_sem=send, recv_sem=recv, device_id=peer,
            device_id_type=pl.DeviceIdType.MESH,
        )

    def span(start, size):
        return pl.ds(pl.multiple_of(start, size), size)

    def partner(r):
        high, low = lax.div(z, 2), lax.rem(z, 2)
        return 2 * (1 - high if r & 2 else high) + (1 - low if r & 1 else low)

    rounds = [r for r in range(scenes - 1, -1, -1)]
    targets = [partner(r) for r in rounds]

    loads = [
        pltpu.make_async_copy(src, dst, load_sem.at[i])
        for i, (src, dst) in enumerate(
            (
                (q_hbm, q_ref), (k_hbm, k_ref), (v_hbm, v_ref), (w_hbm, w_ref),
                (dec_hbm.at[0, 0, span(c * half, half), :], dec_ref),
            )
        )
    ]
    for load in loads:
        load.start()

    barrier = pltpu.get_barrier_semaphore()
    peers = [core_peer, x_peer, y_peer] + [{"scene": targets[j]} for j in range(scenes - 1)]
    for peer in peers:
        pl.semaphore_signal(barrier, inc=1, device_id=peer, device_id_type=pl.DeviceIdType.MESH)
    pl.semaphore_wait(barrier, len(peers))

    def core_copy(j):
        return remote(
            dec_hbm.at[0, 0, span((1 - c) * half, half), span(targets[j] * cols, cols)],
            core_in.at[j], core_send.at[j], core_recv.at[j], core_peer,
        )

    for j in range(scenes):
        core_copy(j).start()

    def forward(h):
        head = slice(h * HEAD_DIM, (h + 1) * HEAD_DIM)
        hidden = jnp.concatenate(
            [
                jnp.concatenate(
                    [
                        jnp.full(
                            (map_block, q_block),
                            jnp.where(mask_ref[0, qb, mb] == 1, 0.0, -1e30),
                            jnp.float32,
                        )
                        for qb in range(q_blocks)
                    ],
                    axis=1,
                )
                for mb in range(map_blocks)
            ],
            axis=0,
        )
        scores = hidden + scaling * lax.dot_general(
            k_ref[0, :, head], q_ref[0, :, head], (((1,), (1,)), ((), ())),
            preferred_element_type=jnp.float32,
        )
        exponent = jnp.exp(scores - jnp.max(scores, axis=0, keepdims=True))
        prob = exponent * (1.0 / jnp.sum(exponent, axis=0, keepdims=True))
        probs[h] = prob
        value = lax.dot_general(
            v_ref[0, :, head], prob.astype(jnp.bfloat16), (((0,), (0,)), ((), ())),
            preferred_element_type=jnp.float32,
        )
        att_all[z, :, head] = value.T.astype(jnp.bfloat16)
        keys_t[h] = k_ref[0, :, head].T

    def add(a, b):
        return (a.astype(jnp.float32) + b.astype(jnp.float32)).astype(jnp.bfloat16)

    def move_attended(step, wait_only):
        for way, sign in ((0, 1), (1, -1)):
            slot = z - sign * step
            there = (slot >= 0) if sign == 1 else (slot < scenes)
            onward = (z < scenes - 1) if sign == 1 else (z > 0)

            @pl.when(jnp.logical_and(there, onward) if step == 0 or wait_only else there)
            def _():
                copy = remote(
                    att_all.at[slot], att_all.at[slot], att_send.at[way, step], att_recv.at[slot],
                    {"scene": z + sign},
                )
                if wait_only:
                    copy.wait_send()
                elif step == 0:
                    copy.start()
                else:
                    copy.wait_recv()
                    pl.when(onward)(lambda: copy.start())

    bits = ((x, y), (y, x))
    order = ((x_peer, y_peer), (y_peer, x_peer))
    starts = [c * half + bits[l][0] * quarter + bits[l][1] * eighth for l in range(2)]
    places = [span(starts[l], eighth) for l in range(2)]

    def half_copy(j, l):
        return remote(
            acc.at[j, l, span((1 - bits[l][0]) * quarter, quarter), :], half_in.at[j, l],
            half_send.at[j, l], half_recv.at[j, l], order[l][0],
        )

    def quarter_copy(j, l):
        return remote(
            acc_half.at[j, l, span((1 - bits[l][1]) * eighth, eighth), :], quarter_in.at[j, l],
            quarter_send.at[j, l], quarter_recv.at[j, l], order[l][1],
        )

    def swap(j, l, slot):
        return remote(
            piece.at[j, l], up.at[slot, l, places[l], :], swap_send.at[j, l], swap_recv.at[j, l],
            {"scene": targets[j]},
        )

    def sum_core(j):
        core_copy(j).wait_recv()
        for l in range(2):
            mine = dec_ref[:, span(targets[j] * cols + l * lane, lane)]
            acc[j, l] = add(mine, core_in[j, :, l * lane : (l + 1) * lane])
            half_copy(j, l).start()

    def sum_half(j):
        for l in range(2):
            half_copy(j, l).wait_recv()
            acc_half[j, l] = add(acc[j, l, span(bits[l][0] * quarter, quarter), :], half_in[j, l])
            quarter_copy(j, l).start()

    def sum_quarter(j):
        for l in range(2):
            quarter_copy(j, l).wait_recv()
            total = add(acc_half[j, l, span(bits[l][1] * eighth, eighth), :], quarter_in[j, l])
            row = starts[l] + lax.broadcasted_iota(jnp.int32, total.shape, 0)
            total = jnp.where(row < count_ref[0], total.astype(jnp.float32), 0.0)
            if j < scenes - 1:
                piece[j, l] = total.astype(jnp.bfloat16)
                swap(j, l, z).start()
            else:
                up[z, l, places[l], :] = total.astype(jnp.bfloat16)

    def gathered(j, l, size, lead, sems, peer):
        ref = up.at[targets[j], l, span(lead, size), :]
        return remote(ref, ref, sems[0].at[j, l], sems[1].at[j, l], peer)

    def gather_one(j, l, away=0):
        bit = 1 - bits[l][1] if away else bits[l][1]
        lead = c * half + bits[l][0] * quarter + bit * eighth
        return gathered(j, l, eighth, lead, (g1_send, g1_recv), order[l][1])

    def gather_two(j, l, away=0):
        bit = 1 - bits[l][0] if away else bits[l][0]
        return gathered(j, l, quarter, c * half + bit * quarter, (g2_send, g2_recv), order[l][0])

    def gather_three(j, away=0):
        core = 1 - c if away else c
        ref = up.at[targets[j], :, span(core * half, half), :]
        return remote(ref, ref, g3_send.at[j], g3_recv.at[j], core_peer)

    def spread_one(j):
        for l in range(2):
            if j < scenes - 1:
                swap(j, l, targets[j]).wait_recv()
            gather_one(j, l).start()

    def spread_two(j):
        for l in range(2):
            gather_one(j, l, 1).wait_recv()
            gather_two(j, l).start()

    def spread_three(j):
        for l in range(2):
            gather_two(j, l, 1).wait_recv()
        gather_three(j).start()

    def part_copy(j, b):
        t = targets[j]
        to = z + jnp.where(t > z, 1, -1)
        slot = jnp.where(jnp.logical_and(to == t, t < z), scenes, t)
        return remote(
            part_out.at[j, b], part_in.at[slot, b], part_send.at[j, b], part_recv.at[slot, b],
            {"scene": to},
        )

    def landed_part(slot, b):
        return remote(
            part_out.at[0, b], part_in.at[slot, b], part_send.at[0, b], part_recv.at[slot, b],
            core_peer,
        )

    share = width // 2
    has_prev = [jnp.where(targets[j] > z, z, scenes - 1 - z) > 0 for j in range(scenes)]

    def multiply(j):
        gather_three(j, 1).wait_recv()
        t = targets[j]
        for b in range(2):
            part = sum(
                lax.dot_general(
                    up[t, l],
                    w_ref[b * share : (b + 1) * share, l * lane : (l + 1) * lane],
                    (((1,), (1,)), ((), ())),
                    preferred_element_type=jnp.float32,
                )
                for l in range(2)
            )
            parts[j, b] = part
            if j < scenes - 1:

                @pl.when(jnp.logical_not(has_prev[j]))
                def _():
                    part_out[j, b] = parts[j, b].astype(jnp.bfloat16)
                    part_copy(j, b).start()

    def merge(j):
        @pl.when(has_prev[j])
        def _():
            for b in range(2):
                landed_part(targets[j], b).wait_recv()
                part_out[j, b] = add(parts[j, b], part_in[targets[j], b])
                part_copy(j, b).start()

    stages = (
        sum_core, sum_half, sum_quarter, spread_one, spread_two, spread_three, multiply
    )
    loads[0].wait()
    loads[1].wait()
    loads[2].wait()
    forward(0)
    loads[4].wait()
    for tick in range(scenes + len(stages) - 1):
        for lag, stage in enumerate(stages):
            if stage is multiply and tick == lag:
                loads[3].wait()
            if 0 <= tick - lag < scenes:
                stage(tick - lag)
        if tick + 1 < heads:
            forward(tick + 1)
        if tick == heads - 2:
            move_attended(0, False)
        if tick == 5:
            move_attended(1, False)
        if tick == 7:
            move_attended(2, False)
        if tick == 8:
            merge(1)
        if tick == 9:
            merge(0)
    merge(2)
    move_attended(scenes - 1, False)

    def weight_columns(tile, carry):
        for l in range(2):
            size = lane // 2
            at = span(tile * size, size)
            dw_ref[:, span(l * lane + tile * size, size)] = sum(
                lax.dot_general(
                    att_all[s], up[s, l, :, at], (((0,), (0,)), ((), ())),
                    preferred_element_type=jnp.float32,
                )
                for s in range(scenes)
            )
        return carry

    lax.fori_loop(0, 2, weight_columns, 0)

    store_dw = pltpu.make_async_copy(dw_ref, dw_hbm, store_sem.at[0])
    store_dw.start()

    def finish(b):
        own = scenes - 1

        @pl.when(z > 0)
        def _():
            landed_part(z, b).wait_recv()
            parts[own, b] = parts[own, b] + part_in[z, b].astype(jnp.float32)

        @pl.when(z < scenes - 1)
        def _():
            landed_part(scenes, b).wait_recv()
            parts[own, b] = parts[own, b] + part_in[scenes, b].astype(jnp.float32)

    def stores(h):
        head = span(h * HEAD_DIM, HEAD_DIM)
        return [
            pltpu.make_async_copy(src.at[0, :, head], dst.at[0, :, head], store_sem.at[1 + 3 * h + i])
            for i, (src, dst) in enumerate(((dq_ref, dq_hbm), (dk_ref, dk_hbm), (dv_ref, dv_hbm)))
        ]

    def backward(h):
        head = slice(h * HEAD_DIM, (h + 1) * HEAD_DIM)
        b, first = h * HEAD_DIM // share, h * HEAD_DIM % share
        grad = parts[scenes - 1, b, :, first : first + HEAD_DIM].astype(jnp.bfloat16)
        prob = probs[h]
        weights = prob.astype(jnp.bfloat16)
        dv_ref[0, :, head] = jnp.dot(
            weights, grad, preferred_element_type=jnp.float32
        ).astype(jnp.bfloat16)
        d_probs = lax.dot_general(
            v_ref[0, :, head], grad, (((1,), (1,)), ((), ())), preferred_element_type=jnp.float32
        )
        delta = jnp.sum(weights.astype(jnp.float32) * d_probs, axis=0, keepdims=True)
        score_grads = (prob * (d_probs - delta)).astype(jnp.bfloat16)
        dk_ref[0, :, head] = (
            scaling * jnp.dot(score_grads, q_ref[0, :, head], preferred_element_type=jnp.float32)
        ).astype(jnp.bfloat16)
        d_query = scaling * jnp.dot(keys_t[h], score_grads, preferred_element_type=jnp.float32)
        dq_ref[0, :, head] = d_query.T.astype(jnp.bfloat16)

    for h in range(heads):
        if h * HEAD_DIM % share == 0:
            finish(h * HEAD_DIM // share)
        backward(h)
        for store in stores(h):
            store.start()

    for step in range(scenes - 1):
        move_attended(step, True)
    for j in range(scenes):
        core_copy(j).wait_send()
        for l in range(2):
            half_copy(j, l).wait_send()
            quarter_copy(j, l).wait_send()
            gather_one(j, l).wait_send()
            gather_two(j, l).wait_send()
            if j < scenes - 1:
                swap(j, l, z).wait_send()
        gather_three(j).wait_send()
        if j < scenes - 1:
            for b in range(2):
                part_copy(j, b).wait_send()
    store_dw.wait()
    for h in range(heads):
        for store in stores(h):
            store.wait()


def fused_shards(scenes, dec_grad, agent_queries, map_keys, map_values, w_out, block_mask, agent_count):
    rows, width = agent_queries.shape[1:]
    map_rows = map_keys.shape[1]
    model = dec_grad.shape[3]
    cols = w_out.shape[1]
    lane = cols // 2
    heads = width // HEAD_DIM
    bf16, f32 = jnp.bfloat16, jnp.float32
    anywhere, smem = pl.BlockSpec(memory_space=pltpu.HBM), pl.BlockSpec(memory_space=pltpu.SMEM)
    dma, vmem = pltpu.SemaphoreType.DMA, pltpu.VMEM
    return pl.pallas_call(
        functools.partial(attention_kernel, scenes),
        out_shape=(
            jax.ShapeDtypeStruct((1, rows, width), bf16),
            jax.ShapeDtypeStruct((1, map_rows, width), bf16),
            jax.ShapeDtypeStruct((1, map_rows, width), bf16),
            jax.ShapeDtypeStruct((width, cols), f32),
        ),
        in_specs=[anywhere] * 5 + [smem] * 2,
        out_specs=(anywhere,) * 4,
        scratch_shapes=[
            vmem((rows // 2, model), bf16),
            vmem((1, rows, width), bf16),
            vmem((1, map_rows, width), bf16),
            vmem((1, map_rows, width), bf16),
            vmem((width, cols), bf16),
            vmem((1, rows, width), bf16),
            vmem((1, map_rows, width), bf16),
            vmem((1, map_rows, width), bf16),
            vmem((width, cols), f32),
            vmem((scenes, rows // 2, cols), bf16),
            vmem((scenes, 2, rows // 2, lane), bf16),
            vmem((scenes, 2, rows // 4, lane), bf16),
            vmem((scenes, 2, rows // 4, lane), bf16),
            vmem((scenes, 2, rows // 8, lane), bf16),
            vmem((scenes, 2, rows // 8, lane), bf16),
            vmem((scenes, 2, rows, lane), bf16),
            vmem((scenes, rows, width), bf16),
            vmem((heads, HEAD_DIM, map_rows), bf16),
            vmem((heads, map_rows, rows), f32),
            vmem((scenes, 2, rows, width // 2), f32),
            vmem((scenes, 2, rows, width // 2), bf16),
            vmem((scenes + 1, 2, rows, width // 2), bf16),
            dma((5,)),
            dma((1 + 3 * heads,)),
            dma((scenes,)),
            dma((scenes,)),
            *[dma((scenes, 2))] * 10,
            dma((scenes,)),
            dma((scenes,)),
            dma((2, scenes)),
            dma((scenes,)),
            dma((scenes, 2)),
            dma((scenes + 1, 2)),
        ],
        compiler_params=pltpu.CompilerParams(
            collective_id=0, has_side_effects=True, vmem_limit_bytes=52 * 1024 * 1024
        ),
    )(dec_grad, agent_queries, map_keys, map_values, w_out, block_mask, agent_count)


def solution(mesh):
    scenes = mesh.shape["scene"]

    def body(dec_grad, agent_queries, map_keys, map_values, w_out, block_mask, agent_count):
        args = (dec_grad, agent_queries, map_keys, map_values, w_out, block_mask, agent_count)
        fits = (
            (mesh.shape["section"], mesh.shape["mp"], dec_grad.shape[1]) == (2, 4, 1)
            and scenes == 4
            and dec_grad.shape[2] % 128 == 0
            and w_out.shape[1] % 512 == 0
            and w_out.shape[0] % 256 == 0
        )
        return functools.partial(fused_shards, scenes)(*args) if fits else shards(*args)

    return jax.shard_map(
        body,
        mesh=mesh,
        in_specs=(
            P("scene", ("section", "mp"), None, None),
            P("scene", None, ("section", "mp")),
            P("scene", None, ("section", "mp")),
            P("scene", None, ("section", "mp")),
            P(("section", "mp"), "scene"),
            P("scene", None, None),
            P("scene"),
        ),
        out_specs=(
            P("scene", None, ("section", "mp")),
            P("scene", None, ("section", "mp")),
            P("scene", None, ("section", "mp")),
            P(("section", "mp"), "scene"),
        ),
        check_vma=False,
    )
```

```python
import functools
import math

import jax
import jax.numpy as jnp
from jax import lax
from jax.experimental import pallas as pl
from jax.experimental.pallas import tpu as pltpu
from jax.sharding import PartitionSpec as P

HEAD_DIM = 128


def attend_forward(query_heads, key_heads, value_heads, visible, scaling):
    scores = (
        jnp.einsum("qhd,khd->hqk", query_heads, key_heads, preferred_element_type=jnp.float32)
        * scaling
    )
    scores = jnp.where(visible[None], scores, -1e30)
    largest = jnp.max(scores, axis=-1, keepdims=True)
    exponent = jnp.exp(scores - largest)
    probs = exponent / jnp.sum(exponent, axis=-1, keepdims=True)
    weights = probs.astype(jnp.bfloat16)
    attended = jnp.einsum("hqk,khd->qhd", weights, value_heads, preferred_element_type=jnp.float32)
    return (probs, weights, attended)


def attend_backward(
    query_heads, key_heads, value_heads, grad_heads, probs, weights, attended, scaling
):
    delta = jnp.sum(grad_heads.astype(jnp.float32) * attended, axis=-1)
    d_values = jnp.einsum(
        "hqk,qhd->khd", weights, grad_heads, preferred_element_type=jnp.float32
    ).astype(jnp.bfloat16)
    d_probs = jnp.einsum(
        "qhd,khd->hqk", grad_heads, value_heads, preferred_element_type=jnp.float32
    )
    score_grads = (probs * (d_probs - delta.T[:, :, None])).astype(jnp.bfloat16)
    d_queries = (
        scaling
        * jnp.einsum("hqk,khd->qhd", score_grads, key_heads, preferred_element_type=jnp.float32)
    ).astype(jnp.bfloat16)
    d_keys = (
        scaling
        * jnp.einsum("hqk,qhd->khd", score_grads, query_heads, preferred_element_type=jnp.float32)
    ).astype(jnp.bfloat16)
    return (d_queries, d_keys, d_values)


def reduce_weights(attended_rounded, upstream):
    term = jnp.einsum("qh,qd->hd", attended_rounded, upstream, preferred_element_type=jnp.float32)
    return lax.psum_scatter(term, "scene", scatter_dimension=1, tiled=True)


def shards(dec_grad, agent_queries, map_keys, map_values, w_out, block_mask, agent_count):
    scaling = 1.0 / math.sqrt(HEAD_DIM)
    partial_sum = jnp.sum(dec_grad[0].astype(jnp.float32), axis=0).astype(jnp.bfloat16)
    agent_total = agent_count[0]
    token_rows = partial_sum.shape[0]
    summed = lax.psum(partial_sum, ("section", "mp")).astype(jnp.float32)
    row_keep = jnp.arange(token_rows) < agent_total
    upstream = jnp.where(row_keep[:, None], summed, 0.0).astype(jnp.bfloat16)
    proj_width = w_out.shape[0]
    d_attn = jnp.einsum(
        "td,hd->th",
        upstream,
        lax.all_gather(w_out, "scene", axis=1, tiled=True),
        preferred_element_type=jnp.float32,
    ).astype(jnp.bfloat16)
    head_count = proj_width // HEAD_DIM
    query_heads = agent_queries[0].reshape(token_rows, head_count, HEAD_DIM)
    grad_heads = d_attn.reshape(token_rows, head_count, HEAD_DIM)
    key_rows = map_keys[0]
    value_rows = map_values[0]
    mask_rows = block_mask[0]
    map_blocks = mask_rows.shape[1]
    block_size = key_rows.shape[0] // map_blocks
    visible = jnp.repeat(jnp.repeat(mask_rows == 1, block_size, axis=0), block_size, axis=1)
    key_heads = key_rows.reshape(-1, head_count, HEAD_DIM)
    value_heads = value_rows.reshape(-1, head_count, HEAD_DIM)
    probs, weights, attended = attend_forward(query_heads, key_heads, value_heads, visible, scaling)
    attended_rounded = attended.astype(jnp.bfloat16).reshape(token_rows, proj_width)
    d_queries, d_keys, d_values = attend_backward(
        query_heads, key_heads, value_heads, grad_heads, probs, weights, attended, scaling
    )
    d_wout = reduce_weights(attended_rounded, upstream)
    d_keys_out = d_keys.reshape(-1, proj_width)
    d_values_out = d_values.reshape(-1, proj_width)
    return (
        d_queries.reshape(token_rows, proj_width)[None],
        d_keys_out[None],
        d_values_out[None],
        d_wout,
    )


def attention_kernel(
    scenes, dec_hbm, q_hbm, k_hbm, v_hbm, w_hbm, mask_ref, count_ref,
    dq_hbm, dk_hbm, dv_hbm, dw_hbm,
    dec_ref, q_ref, k_ref, v_ref, w_ref, dq_ref, dk_ref, dv_ref, dw_ref,
    core_in, acc, plane_in, piece, up, att_all, keys_t, probs, parts, part_out, part_in,
    load_sem, store_sem, core_send, core_recv, plane_send, plane_recv, swap_send, swap_recv,
    gather_send, gather_recv, share_send, share_recv, att_send, att_recv, part_send, part_recv,
):
    z, y, m = lax.axis_index("scene"), lax.axis_index("section"), lax.axis_index("mp")
    x, c = lax.div(m, 2), lax.rem(m, 2)
    core_peer = {"mp": m + 1 - 2 * c}
    chips = [
        {"section": 1 - y if i & 2 else y, "mp": m + 2 - 4 * x if i & 1 else m} for i in range(4)
    ]
    chip = 2 * y + x
    rows_of = [2 * (1 - y if i & 2 else y) + (1 - x if i & 1 else x) for i in range(4)]
    rows, width = q_ref.shape[1], q_ref.shape[2]
    half, eighth = rows // 2, rows // 8
    cols = w_ref.shape[1]
    heads = width // HEAD_DIM
    scaling = 1.0 / math.sqrt(HEAD_DIM)
    map_blocks, q_blocks = mask_ref.shape[2], mask_ref.shape[1]
    map_block, q_block = k_ref.shape[1] // map_blocks, rows // q_blocks

    def remote(src, dst, send, recv, peer):
        return pltpu.make_async_remote_copy(
            src_ref=src, dst_ref=dst, send_sem=send, recv_sem=recv, device_id=peer,
            device_id_type=pl.DeviceIdType.MESH,
        )

    def span(start, size):
        return pl.ds(pl.multiple_of(start, size), size)

    def partner(r):
        high, low = lax.div(z, 2), lax.rem(z, 2)
        return 2 * (1 - high if r & 2 else high) + (1 - low if r & 1 else low)

    rounds = [r for r in range(scenes - 1, -1, -1)]
    targets = [partner(r) for r in rounds]

    loads = [
        pltpu.make_async_copy(src, dst, load_sem.at[i])
        for i, (src, dst) in enumerate(
            (
                (q_hbm, q_ref), (k_hbm, k_ref), (v_hbm, v_ref), (w_hbm, w_ref),
                (dec_hbm.at[0, 0, span(c * half, half), :], dec_ref),
            )
        )
    ]
    for load in loads:
        load.start()

    barrier = pltpu.get_barrier_semaphore()
    peers = [core_peer] + chips[1:] + [{"scene": targets[j]} for j in range(scenes - 1)]
    for peer in peers:
        pl.semaphore_signal(barrier, inc=1, device_id=peer, device_id_type=pl.DeviceIdType.MESH)
    pl.semaphore_wait(barrier, len(peers))

    def core_copy(j):
        return remote(
            dec_hbm.at[0, 0, span((1 - c) * half, half), span(targets[j] * cols, cols)],
            core_in.at[j], core_send.at[j], core_recv.at[j], core_peer,
        )

    core_copy(0).start()

    def forward(h):
        head = slice(h * HEAD_DIM, (h + 1) * HEAD_DIM)
        hidden = jnp.concatenate(
            [
                jnp.concatenate(
                    [
                        jnp.full(
                            (map_block, q_block),
                            jnp.where(mask_ref[0, qb, mb] == 1, 0.0, -1e30),
                            jnp.float32,
                        )
                        for qb in range(q_blocks)
                    ],
                    axis=1,
                )
                for mb in range(map_blocks)
            ],
            axis=0,
        )
        scores = hidden + scaling * lax.dot_general(
            k_ref[0, :, head], q_ref[0, :, head], (((1,), (1,)), ((), ())),
            preferred_element_type=jnp.float32,
        )
        exponent = jnp.exp(scores - jnp.max(scores, axis=0, keepdims=True))
        prob = exponent * (1.0 / jnp.sum(exponent, axis=0, keepdims=True))
        probs[h] = prob
        value = lax.dot_general(
            v_ref[0, :, head], prob.astype(jnp.bfloat16), (((0,), (0,)), ((), ())),
            preferred_element_type=jnp.float32,
        )
        att_all[z, :, head] = value.T.astype(jnp.bfloat16)
        keys_t[h] = k_ref[0, :, head].T

    def add(a, b):
        return (a.astype(jnp.float32) + b.astype(jnp.float32)).astype(jnp.bfloat16)

    def move_attended(step, wait_only):
        for way, sign in ((0, 1), (1, -1)):
            slot = z - sign * step
            there = (slot >= 0) if sign == 1 else (slot < scenes)
            onward = (z < scenes - 1) if sign == 1 else (z > 0)

            @pl.when(jnp.logical_and(there, onward) if step == 0 or wait_only else there)
            def _():
                copy = remote(
                    att_all.at[slot], att_all.at[slot], att_send.at[way, step], att_recv.at[slot],
                    {"scene": z + sign},
                )
                if wait_only:
                    copy.wait_send()
                elif step == 0:
                    copy.start()
                else:
                    copy.wait_recv()
                    pl.when(onward)(lambda: copy.start())

    my_rows = span(c * half + chip * eighth, eighth)

    def plane_copy(j, i):
        return remote(
            acc.at[j, span(rows_of[i] * eighth, eighth), :], plane_in.at[j, i],
            plane_send.at[j, i], plane_recv.at[j, i], chips[i],
        )

    def swap(j, slot):
        return remote(
            piece.at[j], up.at[slot, my_rows, :], swap_send.at[j], swap_recv.at[j],
            {"scene": targets[j]},
        )

    def sum_core(j):
        if j + 1 < scenes:
            core_copy(j + 1).start()
        core_copy(j).wait_recv()
        acc[j] = add(dec_ref[:, span(targets[j] * cols, cols)], core_in[j])
        for i in range(1, 4):
            plane_copy(j, i).start()

    def sum_plane(j):
        total = acc[j, span(chip * eighth, eighth), :].astype(jnp.float32)
        for i in range(1, 4):
            plane_copy(j, i).wait_recv()
            total = total + plane_in[j, i].astype(jnp.float32)
        row = c * half + chip * eighth + lax.broadcasted_iota(jnp.int32, total.shape, 0)
        total = jnp.where(row < count_ref[0], total, 0.0).astype(jnp.bfloat16)
        if j < scenes - 1:
            piece[j] = total
            swap(j, z).start()
        else:
            up[z, my_rows, :] = total

    def gather(j, i, away=0):
        part_rows = span(c * half + rows_of[i if away else 0] * eighth, eighth)
        ref = up.at[targets[j], part_rows, :]
        return remote(ref, ref, gather_send.at[j, i], gather_recv.at[j, i], chips[i])

    def share_core(j, away=0):
        ref = up.at[targets[j], span((1 - c if away else c) * half, half), :]
        return remote(ref, ref, share_send.at[j], share_recv.at[j], core_peer)

    def spread_plane(j):
        if j < scenes - 1:
            swap(j, targets[j]).wait_recv()
        for i in range(1, 4):
            gather(j, i).start()

    def spread_core(j):
        for i in range(1, 4):
            gather(j, i, 1).wait_recv()
        share_core(j).start()

    def part_copy(j, b):
        t = targets[j]
        to = z + jnp.where(t > z, 1, -1)
        slot = jnp.where(jnp.logical_and(to == t, t < z), scenes, t)
        return remote(
            part_out.at[j, b], part_in.at[slot, b], part_send.at[j, b], part_recv.at[slot, b],
            {"scene": to},
        )

    def landed_part(slot, b):
        return remote(
            part_out.at[0, b], part_in.at[slot, b], part_send.at[0, b], part_recv.at[slot, b],
            core_peer,
        )

    has_prev = [jnp.where(targets[j] > z, z, scenes - 1 - z) > 0 for j in range(scenes)]

    def multiply(j):
        share_core(j, 1).wait_recv()
        for two in range(0, heads, 2):
            part = lax.dot_general(
                up[targets[j]], w_ref[two * HEAD_DIM : (two + 2) * HEAD_DIM, :],
                (((1,), (1,)), ((), ())), preferred_element_type=jnp.float32,
            )
            for b in (two, two + 1):
                parts[j, b] = part[:, (b - two) * HEAD_DIM : (b - two + 1) * HEAD_DIM]
            if j < scenes - 1:

                @pl.when(jnp.logical_not(has_prev[j]))
                def _():
                    for b in (two, two + 1):
                        part_out[j, b] = parts[j, b].astype(jnp.bfloat16)
                        part_copy(j, b).start()

    def merge(j):
        @pl.when(has_prev[j])
        def _():
            for b in range(heads):
                landed_part(targets[j], b).wait_recv()
                part_out[j, b] = add(parts[j, b], part_in[targets[j], b])
                part_copy(j, b).start()

    stages = (sum_core, sum_plane, spread_plane, spread_core, multiply)
    for load in loads[:3]:
        load.wait()
    forward(0)
    loads[4].wait()
    for tick in range(scenes + len(stages) - 1):
        for lag, stage in enumerate(stages):
            if stage is multiply and tick == lag:
                loads[3].wait()
            if 0 <= tick - lag < scenes:
                stage(tick - lag)
        if tick == 0:
            forward(1)
        if tick == 1:
            for h in range(2, heads):
                forward(h)
            move_attended(0, False)
        if tick == 4:
            move_attended(1, False)
        if tick == 6:
            move_attended(2, False)
            merge(1)
    merge(0)
    merge(2)
    move_attended(scenes - 1, False)

    def weight_columns(tile, carry):
        at = span(tile * 256, 256)
        dw_ref[:, at] = sum(
            lax.dot_general(
                att_all[s], up[s, :, at], (((0,), (0,)), ((), ())),
                preferred_element_type=jnp.float32,
            )
            for s in range(scenes)
        )
        return carry

    lax.fori_loop(0, cols // 256, weight_columns, 0)

    store_dw = pltpu.make_async_copy(dw_ref, dw_hbm, store_sem.at[0])
    store_dw.start()

    def finish(b):
        own = scenes - 1

        @pl.when(z > 0)
        def _():
            landed_part(z, b).wait_recv()
            parts[own, b] = parts[own, b] + part_in[z, b].astype(jnp.float32)

        @pl.when(z < scenes - 1)
        def _():
            landed_part(scenes, b).wait_recv()
            parts[own, b] = parts[own, b] + part_in[scenes, b].astype(jnp.float32)

    def stores(h):
        head = span(h * HEAD_DIM, HEAD_DIM)
        return [
            pltpu.make_async_copy(src.at[0, :, head], dst.at[0, :, head], store_sem.at[1 + 3 * h + i])
            for i, (src, dst) in enumerate(((dq_ref, dq_hbm), (dk_ref, dk_hbm), (dv_ref, dv_hbm)))
        ]

    def backward(h):
        head = slice(h * HEAD_DIM, (h + 1) * HEAD_DIM)
        grad = parts[scenes - 1, h].astype(jnp.bfloat16)
        prob = probs[h]
        weights = prob.astype(jnp.bfloat16)
        dv_ref[0, :, head] = jnp.dot(
            weights, grad, preferred_element_type=jnp.float32
        ).astype(jnp.bfloat16)
        d_probs = lax.dot_general(
            v_ref[0, :, head], grad, (((1,), (1,)), ((), ())), preferred_element_type=jnp.float32
        )
        delta = jnp.sum(weights.astype(jnp.float32) * d_probs, axis=0, keepdims=True)
        score_grads = (prob * (d_probs - delta)).astype(jnp.bfloat16)
        dk_ref[0, :, head] = (
            scaling * jnp.dot(score_grads, q_ref[0, :, head], preferred_element_type=jnp.float32)
        ).astype(jnp.bfloat16)
        d_query = scaling * jnp.dot(keys_t[h], score_grads, preferred_element_type=jnp.float32)
        dq_ref[0, :, head] = d_query.T.astype(jnp.bfloat16)

    for h in range(heads):
        finish(h)
        backward(h)
        for store in stores(h):
            store.start()

    for step in range(scenes - 1):
        move_attended(step, True)
    for j in range(scenes):
        core_copy(j).wait_send()
        for i in range(1, 4):
            plane_copy(j, i).wait_send()
            gather(j, i).wait_send()
        share_core(j).wait_send()
        if j < scenes - 1:
            swap(j, z).wait_send()
        if j < scenes - 1:
            for b in range(heads):
                part_copy(j, b).wait_send()
    store_dw.wait()
    for h in range(heads):
        for store in stores(h):
            store.wait()


def fused_shards(scenes, dec_grad, agent_queries, map_keys, map_values, w_out, block_mask, agent_count):
    rows, width = agent_queries.shape[1:]
    map_rows = map_keys.shape[1]
    model = dec_grad.shape[3]
    cols = w_out.shape[1]
    heads = width // HEAD_DIM
    bf16, f32 = jnp.bfloat16, jnp.float32
    anywhere, smem = pl.BlockSpec(memory_space=pltpu.HBM), pl.BlockSpec(memory_space=pltpu.SMEM)
    dma, vmem = pltpu.SemaphoreType.DMA, pltpu.VMEM
    return pl.pallas_call(
        functools.partial(attention_kernel, scenes),
        out_shape=(
            jax.ShapeDtypeStruct((1, rows, width), bf16),
            jax.ShapeDtypeStruct((1, map_rows, width), bf16),
            jax.ShapeDtypeStruct((1, map_rows, width), bf16),
            jax.ShapeDtypeStruct((width, cols), f32),
        ),
        in_specs=[anywhere] * 5 + [smem] * 2,
        out_specs=(anywhere,) * 4,
        scratch_shapes=[
            vmem((rows // 2, model), bf16),
            vmem((1, rows, width), bf16),
            vmem((1, map_rows, width), bf16),
            vmem((1, map_rows, width), bf16),
            vmem((width, cols), bf16),
            vmem((1, rows, width), bf16),
            vmem((1, map_rows, width), bf16),
            vmem((1, map_rows, width), bf16),
            vmem((width, cols), f32),
            vmem((scenes, rows // 2, cols), bf16),
            vmem((scenes, rows // 2, cols), bf16),
            vmem((scenes, 4, rows // 8, cols), bf16),
            vmem((scenes, rows // 8, cols), bf16),
            vmem((scenes, rows, cols), bf16),
            vmem((scenes, rows, width), bf16),
            vmem((heads, HEAD_DIM, map_rows), bf16),
            vmem((heads, map_rows, rows), f32),
            vmem((scenes, heads, rows, HEAD_DIM), f32),
            vmem((scenes, heads, rows, HEAD_DIM), bf16),
            vmem((scenes + 1, heads, rows, HEAD_DIM), bf16),
            dma((5,)),
            dma((1 + 3 * heads,)),
            dma((scenes,)),
            dma((scenes,)),
            *[dma((scenes, 4))] * 2,
            *[dma((scenes,))] * 2,
            *[dma((scenes, 4))] * 2,
            *[dma((scenes,))] * 2,
            dma((2, scenes)),
            dma((scenes,)),
            dma((scenes, heads)),
            dma((scenes + 1, heads)),
        ],
        compiler_params=pltpu.CompilerParams(
            collective_id=0, has_side_effects=True, vmem_limit_bytes=62 * 1024 * 1024
        ),
    )(dec_grad, agent_queries, map_keys, map_values, w_out, block_mask, agent_count)


def solution(mesh):
    scenes = mesh.shape["scene"]

    def body(dec_grad, agent_queries, map_keys, map_values, w_out, block_mask, agent_count):
        args = (dec_grad, agent_queries, map_keys, map_values, w_out, block_mask, agent_count)
        fits = (
            (mesh.shape["section"], mesh.shape["mp"], dec_grad.shape[1]) == (2, 4, 1)
            and scenes == 4
            and dec_grad.shape[2] % 128 == 0
            and w_out.shape[1] % 512 == 0
            and w_out.shape[0] % 256 == 0
        )
        return functools.partial(fused_shards, scenes)(*args) if fits else shards(*args)

    return jax.shard_map(
        body,
        mesh=mesh,
        in_specs=(
            P("scene", ("section", "mp"), None, None),
            P("scene", None, ("section", "mp")),
            P("scene", None, ("section", "mp")),
            P("scene", None, ("section", "mp")),
            P(("section", "mp"), "scene"),
            P("scene", None, None),
            P("scene"),
        ),
        out_specs=(
            P("scene", None, ("section", "mp")),
            P("scene", None, ("section", "mp")),
            P("scene", None, ("section", "mp")),
            P(("section", "mp"), "scene"),
        ),
        check_vma=False,
    )
```
